32 devices in a mesh: prow: 4 (over x, core), pcol: 8 (over z, y).
Axes of the slice: x: 2, y: 2, z: 4, core: 2. Of those that a mesh axis runs over, the one named last changes fastest.
Arguments:
- strip_quad: bfloat16 [4, 2048, 192, 128], P('prow', 'pcol'), may hold values from -0.4375 to 0.4375
- strip_weight: float32 [4, 2048, 192], P('prow', 'pcol'), may hold values from 0.25 to 4
- strip_dest: int32 [4, 2048, 1], P('prow', 'pcol'), may hold values from 0 to 7; in each aligned block of 256 rows (0 to 255, 256 to 511, ..., all dimensions but the last counted through in order) at most 48 rows name the same one
- strip_target: int32 [4, 2048], P('prow', 'pcol'), may hold values from 0 to 31
- strip_count: int32 [4, 8], P('prow', 'pcol'), may hold values from 1 to 256, 1536 in all within a row
- inner_quad: bfloat16 [4, 1024, 192, 128], P('prow', 'pcol'), may hold values from -0.4375 to 0.4375
- inner_weight: float32 [4, 1024, 192], P('prow', 'pcol'), may hold values from 0.25 to 4
- inner_target: int32 [4, 1024], P('prow', 'pcol'), may hold values from 0 to 31
- coarse_owner: int32 [4, 256], P('prow', 'pcol'), may hold values from 0 to 3
- panel_shift: float32 [4, 8, 128], P('prow', 'pcol'), may hold values from 2 to 64
Outputs:
- assembled: bfloat16 [4, 256, 128, 128], P('prow', 'pcol')
- coarse_block: float32 [4, 8, 128, 128], P('prow', 'pcol')
- panel_factor: float32 [4, 8, 128, 128], P('prow', 'pcol')
The draws below stay inside these ranges and needn't reach their ends.
Inputs may be any that keep to these rules, and one draw needn't show every extreme that they name: `strip_dest`: in the 256 strip blocks of one subdomain no patch column is named more than 48 times; in some subdomain one is named exactly 48 times. `strip_count`: in each patch row the counts sum to 1536; strip blocks at or past the count are padding.
All inputs are finite; a program needn't handle non-finite values.
Results may differ from the reference program's by a relative error of at most 0.0035.
Values may be sent and summed in bfloat16 or wider, within the bound.
A program may use at most 320 MiB of HBM per device.

```python
import math
import jax
import jax.numpy as jnp
import numpy as np
from jax import lax

WIDTH = 128
QUAD = 192
STRIPS = 256
INNER = 128
SLOTS = 32
CAPACITY = 48
N_PROW = 4
N_PCOL = 8


def set_ends(array, stream_key, low, top_value):
    shape = array.shape
    spot = [jax.random.randint(jax.random.fold_in(stream_key, axis), (), 0, shape[axis]) for axis in range(len(shape))]
    array = array.at[tuple(spot)].set(low)
    longest = shape.index(max(shape))
    spot[longest] = (spot[longest] + 1) % shape[longest]
    return array.at[tuple(spot)].set(top_value)


def block_scale(own_key, dims, shards, low, high):
    def one(dim, parts):
        heights = jax.random.uniform(jax.random.fold_in(jax.random.fold_in(own_key, 6), dim), (parts,), jnp.float32, low / len(shards), high / len(shards))
        return jnp.repeat(jnp.exp(heights), dims[dim] // parts).reshape((-1,) + (1,) * (len(dims) - dim - 1))

    factor_of = one(*shards[0])
    for cut in shards[1:]:
        factor_of = factor_of * one(*cut)
    return factor_of


def length_profile(count, total, most, slope):
    weights = [(1 << 20) // math.isqrt(standing ** slope) + 1 for standing in range(2, count + 1)]
    rest, holding = total - most - (count - 1), [1] * (count - 1)
    while rest > 0:
        candidates = [i for i in range(count - 1) if holding[i] < most]
        pool, remaining = sum([weights[i] for i in candidates]), rest
        for i in candidates:
            extra = min(most - holding[i], max(1, remaining * weights[i] // pool), rest)
            holding[i] = holding[i] + extra
            rest = rest - extra
    return np.array([most] + holding)


def uneven_parts(key, count, total, limit, lean):
    if count == 2:
        one = jax.random.randint(key, (), max(1, total - limit), min(limit, total - 1) + 1)
        return jnp.stack([one, total - one])
    lengths = jnp.asarray(length_profile(count, total, limit, lean), jnp.int32)
    pairs = (count - 1) // 2
    donor, sink = lengths[1:1 + 2 * pairs:2], lengths[2:2 + 2 * pairs:2]
    margin = jnp.minimum(donor - 1, limit - sink)
    shifted = jax.random.randint(jax.random.fold_in(key, 1), (pairs,), 0, 1 << 20) % (margin + 1)
    lengths = lengths.at[1:1 + 2 * pairs:2].set(donor - shifted).at[2:2 + 2 * pairs:2].set(sink + shifted)
    return lengths[jax.random.permutation(jax.random.fold_in(key, 2), count)]


def shared_out(stream_key, own, number, rows, count, top, limit, slope):
    ranking = jax.random.permutation(stream_key, count)
    packed, common = load_shares(count, rows * top, limit, slope, True), load_shares(count, rows * top, limit, slope, False)
    places = jnp.arange(count)

    def named(lengths, offset_by):
        used = int((lengths > 0).sum())
        fixed = max(1, used // 4)
        moved = fixed + (places - fixed + offset_by * (used - fixed)) % max(1, count - fixed)
        return jnp.zeros((count,), jnp.int32).at[ranking[jnp.where(places < fixed, places, moved)]].set(jnp.asarray(lengths, jnp.int32))

    lengths = jnp.where(number % 4 == 0, named(packed, number // 4), named(common, number - number // 4 - 1))
    mixed = jax.random.permutation(jax.random.fold_in(own, 3), count)
    donor, receiver = mixed[0:count // 2 * 2:2], mixed[1:count // 2 * 2:2]
    margin = jnp.minimum(lengths[donor] - 1, limit - lengths[receiver]) // 2
    margin = jnp.where((donor == ranking[0]) | (receiver == ranking[0]) | (lengths[receiver] == 0), 0, jnp.maximum(margin, 0))
    moved = jax.random.randint(jax.random.fold_in(own, 4), (count // 2,), 0, 1 << 20) % (margin + 1)
    lengths = lengths.at[donor].add(-moved).at[receiver].add(moved)
    labels = jnp.searchsorted(jnp.cumsum(lengths), jnp.arange(rows * top), side="right").astype(jnp.int32)
    grid = labels.reshape(top, rows).T
    grid = grid[jax.random.permutation(jax.random.fold_in(own, 1), rows)]
    offset_by = jax.random.randint(jax.random.fold_in(own, 2), (rows, 1), 0, top)
    return jnp.take_along_axis(grid, (jnp.arange(top)[None, :] + offset_by) % top, axis=1)


def load_shares(amount, total, reach, skew, full):
    loads = [(1 << 20) // math.isqrt(rank ** skew) + 1 for rank in range(1, amount + 1)]
    largest = reach if full else min(reach, max(-(-total // amount), total * loads[0] // sum(loads)))
    least = 1 if total - largest >= amount - 1 else 0
    holding, surplus = [largest] + [least] * (amount - 1), total - largest - least * (amount - 1)
    while surplus > 0:
        candidates = [i for i in range(1, amount) if holding[i] < largest] or [i for i in range(1, amount) if holding[i] < reach]
        whole, left = sum([loads[i] for i in candidates]), surplus
        for i in candidates:
            more = min(reach - holding[i], max(1, left * loads[i] // whole), surplus)
            holding[i] = holding[i] + more
            surplus = surplus - more
    return np.array(holding)


def gaussian(key, dims, width, reach, pieces=(), kind=jnp.bfloat16):
    values = width * jax.random.normal(key, dims, jnp.float32)
    if pieces:
        values = values * block_scale(key, dims, pieces, -0.22, 0.18)
    return jnp.clip(values, -reach, reach).astype(kind)


def setup_inputs(seed: int = 0) -> dict:
    seeds = jax.random.split(jax.random.key(seed), 11)
    strip_quad = gaussian(seeds[0], (N_PROW, N_PCOL * STRIPS, QUAD, WIDTH), QUAD ** -0.5, 0.4375, ((0, 4), (1, 8)))
    strip_weight = jnp.clip(jnp.exp(math.log(4.0) - 2.7725887 * jax.random.uniform(seeds[1], (N_PROW, N_PCOL * STRIPS, QUAD), jnp.float32) ** block_scale(seeds[1], (N_PROW, N_PCOL * STRIPS, QUAD), ((0, 4), (1, 8)), -0.2, 0.2)), 0.25, 4.0)
    strip_dest_keys = jax.random.split(jax.random.fold_in(seeds[2], 1), N_PROW * (N_PCOL * STRIPS) // STRIPS)
    strip_dest_turns = jax.random.permutation(jax.random.fold_in(seeds[2], 3), N_PROW * (N_PCOL * STRIPS) // STRIPS)
    strip_dest = jax.vmap(lambda own, number: shared_out(jax.random.fold_in(seeds[2], 2), own, number, STRIPS, N_PCOL, 1, CAPACITY, 2))(strip_dest_keys, strip_dest_turns).reshape((N_PROW, N_PCOL * STRIPS, 1))
    strip_target = set_ends(jax.random.randint(seeds[3], (N_PROW, N_PCOL * STRIPS), 0, SLOTS), jax.random.fold_in(seeds[3], 1), 0, SLOTS - 1).astype(jnp.int32)
    strip_count = jax.vmap(lambda own: uneven_parts(own, N_PCOL, 3 * STRIPS * N_PCOL // 4, STRIPS, 2))(jax.random.split(seeds[4], N_PROW)).reshape((N_PROW, N_PCOL)).astype(jnp.int32)
    inner_quad = gaussian(seeds[5], (N_PROW, N_PCOL * INNER, QUAD, WIDTH), QUAD ** -0.5, 0.4375, ((0, 4), (1, 8)))
    inner_weight = jnp.clip(jnp.exp(math.log(4.0) - 2.7725887 * jax.random.uniform(seeds[6], (N_PROW, N_PCOL * INNER, QUAD), jnp.float32) ** block_scale(seeds[6], (N_PROW, N_PCOL * INNER, QUAD), ((0, 4), (1, 8)), -0.2, 0.2)), 0.25, 4.0)
    inner_target = set_ends(jax.random.randint(seeds[7], (N_PROW, N_PCOL * INNER), 0, SLOTS), jax.random.fold_in(seeds[7], 1), 0, SLOTS - 1).astype(jnp.int32)
    coarse_owner = set_ends(jax.random.randint(seeds[8], (N_PROW, N_PCOL * SLOTS), 0, N_PROW), jax.random.fold_in(seeds[8], 1), 0, N_PROW - 1).astype(jnp.int32)
    panel_shift = jnp.clip(jnp.exp(math.log(64.0) - 3.465736 * jax.random.uniform(seeds[9], (N_PROW, N_PCOL, WIDTH), jnp.float32) ** block_scale(seeds[9], (N_PROW, N_PCOL, WIDTH), ((0, 4), (1, 8)), -0.2, 0.2)), 2.0, 64.0)
    return dict(strip_quad=strip_quad, strip_weight=strip_weight, strip_dest=strip_dest, strip_target=strip_target, strip_count=strip_count, inner_quad=inner_quad, inner_weight=inner_weight, inner_target=inner_target, coarse_owner=coarse_owner, panel_shift=panel_shift)


def tangents(quadrature, weight):
    scaled = (quadrature.astype(jnp.float32) * jnp.sqrt(weight)[..., None]).astype(jnp.bfloat16)
    wide = scaled.astype(jnp.float32)
    return jnp.einsum('nqi,nqj->nij', wide, wide).astype(jnp.bfloat16)

def reference(strip_quad, strip_weight, strip_dest, strip_target, strip_count, inner_quad, inner_weight, inner_target, coarse_owner, panel_shift):

    def one_row(row_items):
        squad, sweight, sdest, starget, scount, iquad, iweight, itarget = row_items
        strip_tangent = tangents(squad, sweight).astype(jnp.float32)
        inner_tangent = tangents(iquad, iweight).astype(jnp.float32)
        strip_index = jnp.arange(N_PCOL * STRIPS, dtype=jnp.int32)
        source_column = strip_index // STRIPS
        valid_rows = strip_index % STRIPS < scount[source_column]
        segment_ids = jnp.where(valid_rows, sdest[:, 0] * SLOTS + starget, N_PCOL * SLOTS).astype(jnp.int32)
        strip_sum = jax.ops.segment_sum(strip_tangent, segment_ids, num_segments=N_PCOL * SLOTS + 1)[:N_PCOL * SLOTS]
        inner_column = jnp.arange(N_PCOL * INNER, dtype=jnp.int32) // INNER
        inner_ids = (inner_column * SLOTS + itarget).astype(jnp.int32)
        inner_sum = jax.ops.segment_sum(inner_tangent, inner_ids, num_segments=N_PCOL * SLOTS)
        return (strip_sum + inner_sum).astype(jnp.bfloat16)
    assembled = lax.map(one_row, (strip_quad, strip_weight, strip_dest, strip_target, strip_count, inner_quad, inner_weight, inner_target))
    slot_column = jnp.arange(N_PCOL * SLOTS, dtype=jnp.int32) // SLOTS
    owner_ids = (slot_column[None, :] * N_PROW + coarse_owner).astype(jnp.int32)
    totals = jax.ops.segment_sum(assembled.reshape(-1, WIDTH, WIDTH).astype(jnp.float32), owner_ids.reshape(-1), num_segments=N_PCOL * N_PROW)
    coarse_block = jnp.transpose(totals.reshape(N_PCOL, N_PROW, WIDTH, WIDTH), (1, 0, 2, 3)) / SLOTS
    lead_block = assembled.reshape(N_PROW, N_PCOL, SLOTS, WIDTH, WIDTH)[:, :, 0].astype(jnp.float32)
    identity = jnp.eye(WIDTH, dtype=jnp.float32)
    panel_matrix = lead_block + coarse_block + identity[None, None] * panel_shift[:, :, None, :]
    panel_factor = jnp.linalg.cholesky(panel_matrix)
    return (assembled, coarse_block, panel_factor)
```

```python
import functools
import jax
import jax.numpy as jnp
from jax import lax
from jax.experimental import pallas as pl
from jax.experimental.pallas import tpu as pltpu
from jax.sharding import PartitionSpec as P

MESH = pl.DeviceIdType.MESH
VMEM_LIMIT = 56 * 1024 * 1024
LANES = 128


def tangent_kernel(group, bucket_ref, weight_ref, quad_ref, out_ref, root, total, stage, sems):
    step = pl.program_id(0)
    buckets = total.shape[0] - 1
    chunk = stage.shape[1]

    @pl.when(step == 0)
    def _():
        root[...] = jnp.sqrt(weight_ref[...])

        @pl.loop(0, buckets + 1)
        def _(k):
            total[k] = jnp.zeros(total.shape[1:], total.dtype)

    @pl.loop(0, group // 8)
    def _(i):
        first = step * group + i * 8
        lane = lax.rem(first, LANES)
        tile = root[:, pl.ds(pl.multiple_of(first - lane, LANES), LANES)]
        tile = pltpu.roll(tile, lax.rem(LANES - lane, LANES), 1)
        for j in range(8):
            scaled = (quad_ref[i * 8 + j].astype(jnp.float32) * tile[:, j : j + 1]).astype(
                jnp.bfloat16
            )
            tangent = lax.dot_general(
                scaled, scaled, (((0,), (0,)), ((), ())), preferred_element_type=jnp.float32
            )
            bucket = bucket_ref[first + j]
            total[bucket] += tangent

    @pl.when(step == pl.num_programs(0) - 1)
    def _():
        copies = []
        for c in range(buckets // chunk):
            if c >= 2:
                copies[c - 2].wait()

            @pl.loop(0, chunk)
            def _(k):
                stage[c % 2, k] = total[c * chunk + k].astype(stage.dtype)

            copies.append(
                pltpu.make_async_copy(
                    stage.at[c % 2], out_ref.at[pl.ds(c * chunk, chunk)], sems.at[c % 2]
                )
            )
            copies[c].start()
        for copy in copies[-2:]:
            copy.wait()


def bucket_sums(quad, weight, bucket, buckets, chunk, dtype):
    count, rows, width = quad.shape
    group = 32
    return pl.pallas_call(
        functools.partial(tangent_kernel, group),
        out_shape=jax.ShapeDtypeStruct((buckets, width, width), dtype),
        grid_spec=pltpu.PrefetchScalarGridSpec(
            num_scalar_prefetch=1,
            grid=(count // group,),
            in_specs=[
                pl.BlockSpec((rows, count), lambda g, b: (0, 0)),
                pl.BlockSpec((group, rows, width), lambda g, b: (g, 0, 0)),
            ],
            out_specs=pl.BlockSpec(memory_space=pl.ANY),
            scratch_shapes=[
                pltpu.VMEM((rows, count), jnp.float32),
                pltpu.VMEM((buckets + 1, width, width), jnp.float32),
                pltpu.VMEM((2, chunk, width, width), dtype),
                pltpu.SemaphoreType.DMA((2,)),
            ],
        ),
        compiler_params=pltpu.CompilerParams(vmem_limit_bytes=VMEM_LIMIT),
    )(bucket, weight.T, quad)


def exchange_kernel(
    outer, inner_size, rows,
    out_ref, inner_ref, pick_ref, shift_ref,
    assembled_ref, coarse_ref, panel_ref,
    own, tot, near, line_out, line_in, part, part_in,
    load_sem, near_send, near_recv, line_send, line_recv, part_send, part_recv,
):
    slots = tot.shape[0]
    width = tot.shape[1]
    row, col = lax.axis_index("prow"), lax.axis_index("pcol")
    a, b = col // inner_size, col % inner_size
    f32 = jnp.float32

    barrier = pltpu.get_barrier_semaphore()

    def greet(r, c):
        pl.semaphore_signal(barrier, inc=1, device_id=(r, c), device_id_type=MESH)

    for j in range(1, inner_size):
        greet(row, a * inner_size + (b + j) % inner_size)
    for j in range(1, rows):
        greet((row + j) % rows, col)

    for j in (1, outer - 1):
        greet(row, (a + j) % outer * inner_size + b)

    pl.semaphore_wait(barrier, inner_size + rows)

    low = a < outer // 2

    def owner(s):
        if s == outer - 1:
            return a
        down = outer - 1 - s
        return jnp.where(
            low,
            jnp.where(down > a, down, down - 1),
            jnp.where(s < a, s, s + 1),
        )

    owners = [owner(s) for s in range(outer)]
    near_copies = []
    for s in range(outer):
        group = []
        for j in range(1, inner_size):
            peer = (b + j) % inner_size
            group.append(
                pltpu.make_async_remote_copy(
                    src_ref=out_ref.at[pl.ds((owners[s] * inner_size + peer) * slots, slots)],
                    dst_ref=near.at[inner_size - j - 1, s],
                    send_sem=near_send.at[inner_size - j - 1, s],
                    recv_sem=near_recv.at[inner_size - j - 1, s],
                    device_id=(row, a * inner_size + peer),
                    device_id_type=MESH,
                )
            )
        near_copies.append(group)
    for group in near_copies:
        for copy in group:
            copy.start()
    loads = [
        pltpu.make_async_copy(
            out_ref.at[pl.ds((owners[s] * inner_size + b) * slots, slots)],
            own.at[s],
            load_sem.at[s],
        )
        for s in range(outer)
    ]
    loads.append(pltpu.make_async_copy(inner_ref, tot, load_sem.at[outer]))
    for load in loads:
        load.start()

    def local(s, k):
        value = own[s, k].astype(f32)
        for j in range(inner_size - 1):
            value = value + near[j, s, k].astype(f32)
        return value

    line_copies = []
    for s in range(outer - 1):
        target = owners[s]
        up = target > a
        way = jnp.where(up, 0, 1)
        after = jnp.where(up, a + 1, a - 1)
        linked = jnp.where(up, a > 0, a < outer - 1)
        copy = pltpu.make_async_remote_copy(
            src_ref=line_out.at[s],
            dst_ref=line_in.at[way, target],
            send_sem=line_send.at[s],
            recv_sem=line_recv.at[way, target],
            device_id=(row, after * inner_size + b),
            device_id_type=MESH,
        )
        loads[s].wait()
        for near_copy in near_copies[s]:
            near_copy.wait_recv()

        @pl.when(linked)
        def _():
            copy.wait_recv()

            @pl.loop(0, slots)
            def _(k):
                value = local(s, k) + line_in[way, target, k].astype(f32)
                line_out[s, k] = value.astype(line_out.dtype)

        @pl.when(jnp.logical_not(linked))
        def _():
            @pl.loop(0, slots)
            def _(k):
                line_out[s, k] = local(s, k).astype(line_out.dtype)

        copy.start()
        line_copies.append(copy)

    last = outer - 1
    loads[last].wait()
    loads[outer].wait()
    for near_copy in near_copies[last]:
        near_copy.wait_recv()

    @pl.loop(0, slots)
    def _(k):
        tot[k] = tot[k] + local(last, k)

    for way, there in ((0, a > 0), (1, a < outer - 1)):

        @pl.when(there)
        def _():
            pltpu.make_async_remote_copy(
                src_ref=line_out.at[0],
                dst_ref=line_in.at[way, a],
                send_sem=line_send.at[0],
                recv_sem=line_recv.at[way, a],
                device_id=(row, a * inner_size + (b + 1) % inner_size),
                device_id_type=MESH,
            ).wait_recv()

            @pl.loop(0, slots)
            def _(k):
                tot[k] = tot[k] + line_in[way, a, k].astype(f32)

    part[...] = jnp.zeros_like(part)

    @pl.loop(0, slots)
    def _(k):
        block = tot[k].astype(jnp.bfloat16)
        assembled_ref[k] = block
        value = block.astype(f32)
        for r in range(rows):
            part[r] += pick_ref[r, k] * value

    part_copies = []
    for j in range(1, rows):
        peer = (row + j) % rows
        part_copies.append(
            pltpu.make_async_remote_copy(
                src_ref=part.at[peer],
                dst_ref=part_in.at[rows - j - 1],
                send_sem=part_send.at[rows - j - 1],
                recv_sem=part_recv.at[rows - j - 1],
                device_id=(peer, col),
                device_id_type=MESH,
            )
        )
    for copy in part_copies:
        copy.start()
    for copy in part_copies:
        copy.wait_recv()
    coarse = part[row]
    for j in range(rows - 1):
        coarse = coarse + part_in[j]
    coarse = coarse / slots
    coarse_ref[...] = coarse
    diagonal = lax.broadcasted_iota(jnp.int32, (width, width), 0) == lax.broadcasted_iota(
        jnp.int32, (width, width), 1
    )
    panel_ref[...] = (
        assembled_ref[0].astype(f32) + coarse + jnp.where(diagonal, shift_ref[...], 0.0)
    )
    for group in near_copies:
        for copy in group:
            copy.wait_send()
    for copy in line_copies + part_copies:
        copy.wait_send()


def exchange(outgoing, inner_sum, pick, shift, columns, rows):
    slots, width, _ = inner_sum.shape
    outer = 4
    inner_size = columns // outer
    f32, bf16 = jnp.float32, jnp.bfloat16
    block = (slots, width, width)
    dma = pltpu.SemaphoreType.DMA
    near = max(1, inner_size - 1)
    line = max(1, outer - 1)
    peers = max(1, rows - 1)
    vmem = pl.BlockSpec(memory_space=pltpu.VMEM)
    return pl.pallas_call(
        functools.partial(exchange_kernel, outer, inner_size, rows),
        out_shape=(
            jax.ShapeDtypeStruct(block, bf16),
            jax.ShapeDtypeStruct((width, width), f32),
            jax.ShapeDtypeStruct((width, width), f32),
        ),
        in_specs=[
            pl.BlockSpec(memory_space=pl.ANY),
            pl.BlockSpec(memory_space=pl.ANY),
            pl.BlockSpec(memory_space=pltpu.SMEM),
            vmem,
        ],
        out_specs=(vmem, vmem, vmem),
        scratch_shapes=[
            pltpu.VMEM((outer,) + block, bf16),
            pltpu.VMEM(block, f32),
            pltpu.VMEM((near, outer) + block, bf16),
            pltpu.VMEM((line,) + block, bf16),
            pltpu.VMEM((2, outer) + block, bf16),
            pltpu.VMEM((rows, width, width), f32),
            pltpu.VMEM((peers, width, width), f32),
            dma((outer + 1,)),
            dma((near, outer)),
            dma((near, outer)),
            dma((line,)),
            dma((2, outer)),
            dma((peers,)),
            dma((peers,)),
        ],
        compiler_params=pltpu.CompilerParams(
            collective_id=0, has_side_effects=True, vmem_limit_bytes=VMEM_LIMIT
        ),
    )(outgoing, inner_sum, pick, shift)


def body(
    strip_quad,
    strip_weight,
    strip_dest,
    strip_target,
    strip_count,
    inner_quad,
    inner_weight,
    inner_target,
    coarse_owner,
    panel_shift,
):
    strip_rows = strip_quad.shape[1]
    width = strip_quad.shape[3]
    slot_total = coarse_owner.shape[1]
    columns = lax.axis_size("pcol")
    row_total = lax.axis_size("prow")
    buckets = columns * slot_total
    position = jnp.arange(strip_rows, dtype=jnp.int32)
    bucket = jnp.where(
        position < strip_count[0, 0], strip_dest[0, :, 0] * slot_total + strip_target[0], buckets
    )
    outgoing = bucket_sums(
        strip_quad[0], strip_weight[0], bucket, buckets, slot_total, jnp.bfloat16
    )
    inner_sum = bucket_sums(
        inner_quad[0], inner_weight[0], inner_target[0], slot_total, slot_total // 2, jnp.float32
    )
    pick = (jnp.arange(row_total, dtype=jnp.int32)[:, None] == coarse_owner[0][None, :]).astype(
        jnp.float32
    )
    assembled, coarse, panel_matrix = exchange(
        outgoing, inner_sum, pick, panel_shift[0], columns, row_total
    )
    factor = jnp.linalg.cholesky(panel_matrix)
    return (
        assembled.reshape(1, slot_total, width, width),
        coarse.reshape(1, 1, width, width),
        factor.reshape(1, 1, width, width),
    )


def solution(mesh):
    placed = (
        P("prow", "pcol", None, None),
        P("prow", "pcol", None),
        P("prow", "pcol", None),
        P("prow", "pcol"),
        P("prow", "pcol"),
        P("prow", "pcol", None, None),
        P("prow", "pcol", None),
        P("prow", "pcol"),
        P("prow", "pcol"),
        P("prow", "pcol", None),
    )
    return jax.shard_map(
        body,
        mesh=mesh,
        in_specs=placed,
        out_specs=(
            P("prow", "pcol", None, None),
            P("prow", "pcol", None, None),
            P("prow", "pcol", None, None),
        ),
        check_vma=False,
    )
```

```python
import functools
import jax
import jax.numpy as jnp
from jax import lax
from jax.experimental import pallas as pl
from jax.experimental.pallas import tpu as pltpu
from jax.sharding import PartitionSpec as P

MESH = pl.DeviceIdType.MESH
VMEM_LIMIT = 60 * 1024 * 1024
UNROLL = 8


def grouped(member, target, valid, groups, capacity, slots):
    count = member.shape[0]
    place = jnp.arange(count, dtype=jnp.int32)
    key = target * count + place
    peer = (member[:, None] == member[None, :]) & valid[None, :]
    rank = jnp.sum((peer & (key[None, :] < key[:, None])).astype(jnp.int32), axis=1)
    spot = jnp.where(valid, member * capacity + rank, groups * capacity)
    at = spot[None, :] == jnp.arange(groups * capacity, dtype=jnp.int32)[:, None]
    packed = jnp.sum(jnp.where(at, key[None, :], 0), axis=1).reshape(groups, capacity)
    order, label = packed % count, packed // count
    same = jnp.concatenate(
        [jnp.zeros((groups, 1), jnp.bool_), label[:, 1:] == label[:, :-1]], axis=1
    ).astype(jnp.float32)
    bucket = jnp.where(valid, member * slots + target, groups * slots)
    index = jnp.arange(groups * slots, dtype=jnp.int32)[:, None]
    held = jnp.sum((bucket[None, :] == index).astype(jnp.int32), axis=1)
    upto = jnp.sum(
        ((bucket[None, :] <= index) & (bucket[None, :] >= index // slots * slots)).astype(
            jnp.int32
        ),
        axis=1,
    )
    last = jnp.maximum(upto - 1, 0).reshape(groups, slots)
    some = (held > 0).astype(jnp.float32).reshape(groups, slots)
    return order, same, last, some


def exchange_kernel(
    outer, inner_size, rows,
    strip_ref, inner_ref, strip_root, inner_root,
    strip_order, strip_same, strip_last, strip_some,
    inner_order, inner_same, inner_last, inner_some,
    pick_ref, shift_ref,
    assembled_ref, coarse_ref, panel_ref,
    quad, run, out, tot, near, line_out, line_in, part, part_in,
    load_sem, near_send, near_recv, line_send, line_recv, part_send, part_recv,
):
    slots = tot.shape[0]
    width = tot.shape[1]
    load = pltpu.make_async_copy(strip_ref, quad, load_sem.at[0])
    load.start()
    row, col = lax.axis_index("prow"), lax.axis_index("pcol")
    a, b = col // inner_size, col % inner_size
    f32 = jnp.float32

    barrier = pltpu.get_barrier_semaphore()

    def greet(r, c):
        pl.semaphore_signal(barrier, inc=1, device_id=(r, c), device_id_type=MESH)

    for j in range(1, inner_size):
        greet(row, a * inner_size + (b + j) % inner_size)
    for j in range(1, rows):
        greet((row + j) % rows, col)

    for j in (1, outer - 1):
        greet(row, (a + j) % outer * inner_size + b)

    pl.semaphore_wait(barrier, inner_size + rows)

    low = a < outer // 2

    def owner(s):
        if s == outer - 1:
            return a
        down = outer - 1 - s
        return jnp.where(
            low,
            jnp.where(down > a, down, down - 1),
            jnp.where(s < a, s, s + 1),
        )

    owners = [owner(s) for s in range(outer)]

    def sum_runs(root, order, same, g):
        def step(i, total):
            for j in range(UNROLL):
                p = i * UNROLL + j
                n = order[g, p]
                scaled = (quad[n].T.astype(f32) * root[n]).astype(jnp.bfloat16)
                tangent = lax.dot_general(
                    scaled, scaled, (((1,), (1,)), ((), ())), preferred_element_type=f32
                )
                total = total * same[g, p] + tangent
                run[p] = total
            return total

        lax.fori_loop(0, order.shape[1] // UNROLL, step, jnp.zeros((width, width), f32))

    load.wait()
    near_copies = []
    for s in range(outer):
        group = []
        for j in range(1, inner_size):
            peer = (b + j) % inner_size
            target = owners[s] * inner_size + peer
            sum_runs(strip_root, strip_order, strip_same, target)

            @pl.loop(0, slots)
            def _(k):
                value = run[strip_last[target, k]] * strip_some[target, k]
                out[j - 1, s, k] = value.astype(out.dtype)

            copy = pltpu.make_async_remote_copy(
                src_ref=out.at[j - 1, s],
                dst_ref=near.at[inner_size - j - 1, s],
                send_sem=near_send.at[inner_size - j - 1, s],
                recv_sem=near_recv.at[inner_size - j - 1, s],
                device_id=(row, a * inner_size + peer),
                device_id_type=MESH,
            )
            copy.start()
            group.append(copy)
        near_copies.append(group)

    def local(s, k):
        mine = owners[s] * inner_size + b
        value = run[strip_last[mine, k]] * strip_some[mine, k]
        for j in range(inner_size - 1):
            value = value + near[j, s, k].astype(f32)
        return value

    line_copies = []
    for s in range(outer - 1):
        target = owners[s]
        up = target > a
        way = jnp.where(up, 0, 1)
        after = jnp.where(up, a + 1, a - 1)
        linked = jnp.where(up, a > 0, a < outer - 1)
        copy = pltpu.make_async_remote_copy(
            src_ref=line_out.at[s],
            dst_ref=line_in.at[way, target],
            send_sem=line_send.at[s],
            recv_sem=line_recv.at[way, target],
            device_id=(row, after * inner_size + b),
            device_id_type=MESH,
        )
        sum_runs(strip_root, strip_order, strip_same, target * inner_size + b)
        for near_copy in near_copies[s]:
            near_copy.wait_recv()

        @pl.when(linked)
        def _():
            copy.wait_recv()

            @pl.loop(0, slots)
            def _(k):
                value = local(s, k) + line_in[way, target, k].astype(f32)
                line_out[s, k] = value.astype(line_out.dtype)

        @pl.when(jnp.logical_not(linked))
        def _():
            @pl.loop(0, slots)
            def _(k):
                line_out[s, k] = local(s, k).astype(line_out.dtype)

        copy.start()
        line_copies.append(copy)

    last = outer - 1
    sum_runs(strip_root, strip_order, strip_same, col)

    @pl.loop(0, slots)
    def _(k):
        tot[k] = run[strip_last[col, k]] * strip_some[col, k]

    load = pltpu.make_async_copy(inner_ref, quad.at[pl.ds(0, inner_ref.shape[0])], load_sem.at[1])
    load.start()
    load.wait()

    @pl.loop(0, inner_order.shape[0])
    def _(g):
        sum_runs(inner_root, inner_order, inner_same, g)

        @pl.loop(0, slots)
        def _(k):
            tot[k] += run[inner_last[g, k]] * inner_some[g, k]

    for near_copy in near_copies[last]:
        near_copy.wait_recv()

    @pl.loop(0, slots)
    def _(k):
        for j in range(inner_size - 1):
            tot[k] += near[j, last, k].astype(f32)

    for way, there in ((0, a > 0), (1, a < outer - 1)):

        @pl.when(there)
        def _():
            pltpu.make_async_remote_copy(
                src_ref=line_out.at[0],
                dst_ref=line_in.at[way, a],
                send_sem=line_send.at[0],
                recv_sem=line_recv.at[way, a],
                device_id=(row, a * inner_size + (b + 1) % inner_size),
                device_id_type=MESH,
            ).wait_recv()

            @pl.loop(0, slots)
            def _(k):
                tot[k] = tot[k] + line_in[way, a, k].astype(f32)

    part[...] = jnp.zeros_like(part)

    @pl.loop(0, slots)
    def _(k):
        block = tot[k].astype(jnp.bfloat16)
        assembled_ref[k] = block
        value = block.astype(f32)
        for r in range(rows):
            part[r] += pick_ref[r, k] * value

    part_copies = []
    for j in range(1, rows):
        peer = (row + j) % rows
        part_copies.append(
            pltpu.make_async_remote_copy(
                src_ref=part.at[peer],
                dst_ref=part_in.at[rows - j - 1],
                send_sem=part_send.at[rows - j - 1],
                recv_sem=part_recv.at[rows - j - 1],
                device_id=(peer, col),
                device_id_type=MESH,
            )
        )
    for copy in part_copies:
        copy.start()
    for copy in part_copies:
        copy.wait_recv()
    coarse = part[row]
    for j in range(rows - 1):
        coarse = coarse + part_in[j]
    coarse = coarse / slots
    coarse_ref[...] = coarse
    diagonal = lax.broadcasted_iota(jnp.int32, (width, width), 0) == lax.broadcasted_iota(
        jnp.int32, (width, width), 1
    )
    panel_ref[...] = (
        assembled_ref[0].astype(f32) + coarse + jnp.where(diagonal, shift_ref[...], 0.0)
    )
    for group in near_copies:
        for copy in group:
            copy.wait_send()
    for copy in line_copies + part_copies:
        copy.wait_send()


def exchange(quads, roots, strip_plan, inner_plan, pick, shift, columns, rows):
    slots = pick.shape[1]
    width = shift.shape[1]
    longest = max(strip_plan[0].shape[1], inner_plan[0].shape[1])
    outer = 4
    inner_size = columns // outer
    f32, bf16 = jnp.float32, jnp.bfloat16
    block = (slots, width, width)
    dma = pltpu.SemaphoreType.DMA
    near = max(1, inner_size - 1)
    line = max(1, outer - 1)
    peers = max(1, rows - 1)
    vmem = pl.BlockSpec(memory_space=pltpu.VMEM)
    return pl.pallas_call(
        functools.partial(exchange_kernel, outer, inner_size, rows),
        out_shape=(
            jax.ShapeDtypeStruct(block, bf16),
            jax.ShapeDtypeStruct((width, width), f32),
            jax.ShapeDtypeStruct((width, width), f32),
        ),
        in_specs=[
            pl.BlockSpec(memory_space=pl.ANY),
            pl.BlockSpec(memory_space=pl.ANY),
            vmem,
            vmem,
        ]
        + [pl.BlockSpec(memory_space=pltpu.SMEM)] * 9
        + [vmem],
        out_specs=(vmem, vmem, vmem),
        scratch_shapes=[
            pltpu.VMEM(quads[0].shape, bf16),
            pltpu.VMEM((longest, width, width), f32),
            pltpu.VMEM((near, outer) + block, bf16),
            pltpu.VMEM(block, f32),
            pltpu.VMEM((near, outer) + block, bf16),
            pltpu.VMEM((line,) + block, bf16),
            pltpu.VMEM((2, outer) + block, bf16),
            pltpu.VMEM((rows, width, width), f32),
            pltpu.VMEM((peers, width, width), f32),
            dma((2,)),
            dma((near, outer)),
            dma((near, outer)),
            dma((line,)),
            dma((2, outer)),
            dma((peers,)),
            dma((peers,)),
        ],
        compiler_params=pltpu.CompilerParams(
            collective_id=0, has_side_effects=True, vmem_limit_bytes=VMEM_LIMIT
        ),
    )(*quads, *roots, *strip_plan, *inner_plan, pick, shift)


def body(
    strip_quad,
    strip_weight,
    strip_dest,
    strip_target,
    strip_count,
    inner_quad,
    inner_weight,
    inner_target,
    coarse_owner,
    panel_shift,
):
    strip_rows = strip_quad.shape[1]
    width = strip_quad.shape[3]
    slot_total = coarse_owner.shape[1]
    columns = lax.axis_size("pcol")
    row_total = lax.axis_size("prow")
    inner_rows = inner_quad.shape[1]
    position = jnp.arange(strip_rows, dtype=jnp.int32)
    strip_plan = grouped(
        strip_dest[0, :, 0],
        strip_target[0],
        position < strip_count[0, 0],
        columns,
        3 * strip_rows // (2 * columns),
        slot_total,
    )
    pieces = 4
    piece = inner_rows // pieces
    position = jnp.arange(inner_rows, dtype=jnp.int32)
    inner_plan = grouped(
        position // piece, inner_target[0], position >= 0, pieces, piece, slot_total
    )
    roots = tuple(jnp.sqrt(weight[0])[:, None, :] for weight in (strip_weight, inner_weight))
    pick = (jnp.arange(row_total, dtype=jnp.int32)[:, None] == coarse_owner[0][None, :]).astype(
        jnp.float32
    )
    assembled, coarse, panel_matrix = exchange(
        (strip_quad[0], inner_quad[0]), roots, strip_plan, inner_plan, pick, panel_shift[0],
        columns, row_total,
    )
    factor = jnp.linalg.cholesky(panel_matrix)
    return (
        assembled.reshape(1, slot_total, width, width),
        coarse.reshape(1, 1, width, width),
        factor.reshape(1, 1, width, width),
    )


def solution(mesh):
    placed = (
        P("prow", "pcol", None, None),
        P("prow", "pcol", None),
        P("prow", "pcol", None),
        P("prow", "pcol"),
        P("prow", "pcol"),
        P("prow", "pcol", None, None),
        P("prow", "pcol", None),
        P("prow", "pcol"),
        P("prow", "pcol"),
        P("prow", "pcol", None),
    )
    return jax.shard_map(
        body,
        mesh=mesh,
        in_specs=placed,
        out_specs=(
            P("prow", "pcol", None, None),
            P("prow", "pcol", None, None),
            P("prow", "pcol", None, None),
        ),
        check_vma=False,
    )
```

```python
import functools
import jax
import jax.numpy as jnp
from jax import lax
from jax.experimental import pallas as pl
from jax.experimental.pallas import tpu as pltpu
from jax.sharding import PartitionSpec as P

MESH = pl.DeviceIdType.MESH
VMEM_LIMIT = 60 * 1024 * 1024
UNROLL = 8
SPAN = 1024


def grouped(member, target, valid, groups, capacity, slots):
    count = member.shape[0]
    place = jnp.arange(count, dtype=jnp.int32)
    key = target * SPAN + place
    peer = (member[:, None] == member[None, :]) & valid[None, :]
    rank = jnp.sum((peer & (key[None, :] < key[:, None])).astype(jnp.int32), axis=1)
    spot = jnp.where(valid, member * capacity + rank, groups * capacity)
    at = spot[None, :] == jnp.arange(groups * capacity, dtype=jnp.int32)[:, None]
    packed = jnp.sum(jnp.where(at, key[None, :], 0), axis=1).reshape(groups, capacity)
    bucket = jnp.where(valid, member * slots + target, groups * slots)[None, None, :]
    index = jnp.arange(groups * slots, dtype=jnp.int32).reshape(groups, slots, 1)
    first = jnp.arange(groups, dtype=jnp.int32)[:, None, None] * slots
    at_or_before = (bucket <= index) & (bucket >= first)
    coded = at_or_before.astype(jnp.int32) + (bucket == index).astype(jnp.int32) * SPAN
    coded = jnp.sum(coded, axis=2)
    last = jnp.where(coded >= SPAN, coded % SPAN - 1, -1)
    return packed, last


def exchange_kernel(
    outer, inner_size, rows, capacity, pieces,
    strip_ref, inner_ref, strip_root, inner_root,
    order_ref, last_ref, owner_ref, shift_ref,
    assembled_ref, coarse_ref, panel_ref,
    quad, run, out, tot, near, line_out, line_in, part, part_in,
    load_sem, near_send, near_recv, line_send, line_recv, part_send, part_recv,
):
    slots = tot.shape[0]
    width = tot.shape[1]
    load = pltpu.make_async_copy(strip_ref, quad, load_sem.at[0])
    load.start()
    row, col = lax.axis_index("prow"), lax.axis_index("pcol")
    a, b = col // inner_size, col % inner_size
    f32 = jnp.float32

    barrier = pltpu.get_barrier_semaphore()

    def greet(r, c):
        pl.semaphore_signal(barrier, inc=1, device_id=(r, c), device_id_type=MESH)

    for j in range(1, inner_size):
        greet(row, a * inner_size + (b + j) % inner_size)
    for j in range(1, rows):
        greet((row + j) % rows, col)

    for j in (1, outer - 1):
        greet(row, (a + j) % outer * inner_size + b)

    pl.semaphore_wait(barrier, inner_size + rows)

    low = a < outer // 2

    def owner(s):
        if s == outer - 1:
            return a
        down = outer - 1 - s
        return jnp.where(
            low,
            jnp.where(down > a, down, down - 1),
            jnp.where(s < a, s, s + 1),
        )

    owners = [owner(s) for s in range(outer)]

    def sum_runs(root, base, length, g):
        def step(i, carry):
            total, before = carry
            for j in range(UNROLL):
                p = i * UNROLL + j
                key = order_ref[g, p]
                n = jnp.maximum(key % SPAN - base, 0)
                label = key // SPAN
                scaled = (quad[n].T.astype(f32) * jnp.sqrt(root[n])).astype(jnp.bfloat16)
                tangent = lax.dot_general(
                    scaled, scaled, (((1,), (1,)), ((), ())), preferred_element_type=f32
                )
                total = total * (label == before).astype(f32) + tangent
                run[p] = total
                before = label
            return total, before

        start = (jnp.zeros((width, width), f32), jnp.int32(-1))
        lax.fori_loop(0, length // UNROLL, step, start)

    def slot_sum(g, k):
        end = last_ref[g, k]
        return run[jnp.maximum(end, 0)] * (end >= 0).astype(f32)

    @pl.when(a == 0)
    def _():
        line_in[0, a] = jnp.zeros(line_in.shape[2:], line_in.dtype)

    @pl.when(a == outer - 1)
    def _():
        line_in[1, a] = jnp.zeros(line_in.shape[2:], line_in.dtype)

    load.wait()
    near_copies = []
    for s in range(outer):
        group = []
        for j in range(1, inner_size):
            peer = (b + j) % inner_size
            target = owners[s] * inner_size + peer
            sum_runs(strip_root, 0, capacity, target)

            @pl.loop(0, slots)
            def _(k):
                out[j - 1, s, k] = slot_sum(target, k).astype(out.dtype)

            copy = pltpu.make_async_remote_copy(
                src_ref=out.at[j - 1, s],
                dst_ref=near.at[inner_size - j - 1, s],
                send_sem=near_send.at[inner_size - j - 1, s],
                recv_sem=near_recv.at[inner_size - j - 1, s],
                device_id=(row, a * inner_size + peer),
                device_id_type=MESH,
            )
            copy.start()
            group.append(copy)
        near_copies.append(group)

    def local(s, k):
        value = slot_sum(owners[s] * inner_size + b, k)
        for j in range(inner_size - 1):
            value = value + near[j, s, k].astype(f32)
        return value

    line_copies = []
    for s in range(outer - 1):
        target = owners[s]
        up = target > a
        way = jnp.where(up, 0, 1)
        after = jnp.where(up, a + 1, a - 1)
        linked = jnp.where(up, a > 0, a < outer - 1)
        copy = pltpu.make_async_remote_copy(
            src_ref=line_out.at[s],
            dst_ref=line_in.at[way, target],
            send_sem=line_send.at[s],
            recv_sem=line_recv.at[way, target],
            device_id=(row, after * inner_size + b),
            device_id_type=MESH,
        )
        sum_runs(strip_root, 0, capacity, target * inner_size + b)
        for near_copy in near_copies[s]:
            near_copy.wait_recv()

        @pl.when(linked)
        def _():
            copy.wait_recv()

            @pl.loop(0, slots)
            def _(k):
                value = local(s, k) + line_in[way, target, k].astype(f32)
                line_out[s, k] = value.astype(line_out.dtype)

        @pl.when(jnp.logical_not(linked))
        def _():
            @pl.loop(0, slots)
            def _(k):
                line_out[s, k] = local(s, k).astype(line_out.dtype)

        copy.start()
        line_copies.append(copy)

    last = outer - 1
    sum_runs(strip_root, 0, capacity, col)

    @pl.loop(0, slots)
    def _(k):
        tot[k] = slot_sum(col, k)

    load = pltpu.make_async_copy(inner_ref, quad.at[pl.ds(0, inner_ref.shape[0])], load_sem.at[1])
    load.start()
    load.wait()

    columns = outer * inner_size

    @pl.loop(columns, columns + pieces)
    def _(g):
        sum_runs(inner_root, strip_ref.shape[0], inner_ref.shape[0] // pieces, g)

        @pl.loop(0, slots)
        def _(k):
            tot[k] += slot_sum(g, k)

    part[...] = jnp.zeros_like(part)

    for way, there in ((0, a > 0), (1, a < outer - 1)):

        @pl.when(there)
        def _():
            pltpu.make_async_remote_copy(
                src_ref=line_out.at[0],
                dst_ref=line_in.at[way, a],
                send_sem=line_send.at[0],
                recv_sem=line_recv.at[way, a],
                device_id=(row, a * inner_size + (b + 1) % inner_size),
                device_id_type=MESH,
            ).wait_recv()

    for near_copy in near_copies[last]:
        near_copy.wait_recv()

    @pl.loop(0, slots)
    def _(k):
        value = tot[k] + line_in[0, a, k].astype(f32) + line_in[1, a, k].astype(f32)
        for j in range(inner_size - 1):
            value = value + near[j, last, k].astype(f32)
        block = value.astype(jnp.bfloat16)
        assembled_ref[k] = block
        value = block.astype(f32)
        for r in range(rows):
            part[r] += (owner_ref[0, k] == r).astype(f32) * value

    part_copies = []
    for j in range(1, rows):
        peer = (row + j) % rows
        part_copies.append(
            pltpu.make_async_remote_copy(
                src_ref=part.at[peer],
                dst_ref=part_in.at[rows - j - 1],
                send_sem=part_send.at[rows - j - 1],
                recv_sem=part_recv.at[rows - j - 1],
                device_id=(peer, col),
                device_id_type=MESH,
            )
        )
    for copy in part_copies:
        copy.start()
    for copy in part_copies:
        copy.wait_recv()
    coarse = part[row]
    for j in range(rows - 1):
        coarse = coarse + part_in[j]
    coarse = coarse / slots
    coarse_ref[...] = coarse
    diagonal = lax.broadcasted_iota(jnp.int32, (width, width), 0) == lax.broadcasted_iota(
        jnp.int32, (width, width), 1
    )
    panel_ref[...] = (
        assembled_ref[0].astype(f32) + coarse + jnp.where(diagonal, shift_ref[...], 0.0)
    )
    for group in near_copies:
        for copy in group:
            copy.wait_send()
    for copy in line_copies + part_copies:
        copy.wait_send()


def exchange(quads, weights, plan, owner, shift, capacity, pieces, columns, rows):
    slots = owner.shape[1]
    width = shift.shape[1]
    longest = plan[0].shape[1]
    outer = 4
    inner_size = columns // outer
    f32, bf16 = jnp.float32, jnp.bfloat16
    block = (slots, width, width)
    dma = pltpu.SemaphoreType.DMA
    near = max(1, inner_size - 1)
    line = max(1, outer - 1)
    peers = max(1, rows - 1)
    vmem = pl.BlockSpec(memory_space=pltpu.VMEM)
    return pl.pallas_call(
        functools.partial(exchange_kernel, outer, inner_size, rows, capacity, pieces),
        out_shape=(
            jax.ShapeDtypeStruct(block, bf16),
            jax.ShapeDtypeStruct((width, width), f32),
            jax.ShapeDtypeStruct((width, width), f32),
        ),
        in_specs=[
            pl.BlockSpec(memory_space=pl.ANY),
            pl.BlockSpec(memory_space=pl.ANY),
            vmem,
            vmem,
        ]
        + [pl.BlockSpec(memory_space=pltpu.SMEM)] * 3
        + [vmem],
        out_specs=(vmem, vmem, vmem),
        scratch_shapes=[
            pltpu.VMEM(quads[0].shape, bf16),
            pltpu.VMEM((longest, width, width), f32),
            pltpu.VMEM((near, outer) + block, bf16),
            pltpu.VMEM(block, f32),
            pltpu.VMEM((near, outer) + block, bf16),
            pltpu.VMEM((line,) + block, bf16),
            pltpu.VMEM((2, outer) + block, bf16),
            pltpu.VMEM((rows, width, width), f32),
            pltpu.VMEM((peers, width, width), f32),
            dma((2,)),
            dma((near, outer)),
            dma((near, outer)),
            dma((line,)),
            dma((2, outer)),
            dma((peers,)),
            dma((peers,)),
        ],
        compiler_params=pltpu.CompilerParams(
            collective_id=0, has_side_effects=True, vmem_limit_bytes=VMEM_LIMIT
        ),
    )(*quads, *weights, *plan, owner, shift)


def body(
    strip_quad,
    strip_weight,
    strip_dest,
    strip_target,
    strip_count,
    inner_quad,
    inner_weight,
    inner_target,
    coarse_owner,
    panel_shift,
):
    strip_rows = strip_quad.shape[1]
    width = strip_quad.shape[3]
    slot_total = coarse_owner.shape[1]
    columns = lax.axis_size("pcol")
    row_total = lax.axis_size("prow")
    inner_rows = inner_quad.shape[1]
    pieces = 4
    piece = inner_rows // pieces
    capacity = 3 * strip_rows // (2 * columns)
    position = jnp.arange(strip_rows, dtype=jnp.int32)
    place = jnp.arange(inner_rows, dtype=jnp.int32)
    plan = grouped(
        jnp.concatenate([strip_dest[0, :, 0], columns + place // piece]),
        jnp.concatenate([strip_target[0], inner_target[0]]),
        jnp.concatenate([position < strip_count[0, 0], place >= 0]),
        columns + pieces,
        max(capacity, piece),
        slot_total,
    )
    weights = tuple(weight[0][:, None, :] for weight in (strip_weight, inner_weight))
    assembled, coarse, panel_matrix = exchange(
        (strip_quad[0], inner_quad[0]), weights, plan, coarse_owner, panel_shift[0],
        capacity, pieces, columns, row_total,
    )
    factor = lax.linalg.cholesky(panel_matrix, symmetrize_input=False)
    return (
        assembled.reshape(1, slot_total, width, width),
        coarse.reshape(1, 1, width, width),
        factor.reshape(1, 1, width, width),
    )


def solution(mesh):
    placed = (
        P("prow", "pcol", None, None),
        P("prow", "pcol", None),
        P("prow", "pcol", None),
        P("prow", "pcol"),
        P("prow", "pcol"),
        P("prow", "pcol", None, None),
        P("prow", "pcol", None),
        P("prow", "pcol"),
        P("prow", "pcol"),
        P("prow", "pcol", None),
    )
    return jax.shard_map(
        body,
        mesh=mesh,
        in_specs=placed,
        out_specs=(
            P("prow", "pcol", None, None),
            P("prow", "pcol", None, None),
            P("prow", "pcol", None, None),
        ),
        check_vma=False,
    )
```
